32 devices in a mesh: dp: 8 (over z, y), tensor: 4 (over x, core).
Axes of the slice: x: 2, y: 2, z: 4, core: 2. Of those that a mesh axis runs over, the one named last changes fastest.
Arguments:
- tokens: bfloat16 [16384, 1024], P(('dp', 'tensor')), may hold values from -6 to 6
- w_in: bfloat16 [1024, 3, 1024], P(None, None, 'tensor'), may hold values from -0.1875 to 0.1875
- conv_kernel: bfloat16 [3, 1024], P(None, 'tensor'), may hold values from -3.5 to 3.5
- w_out: bfloat16 [1024, 1024], P('tensor'), may hold values from -0.1875 to 0.1875
- w_gate: bfloat16 [1024, 4608], P(None, 'tensor'), may hold values from -0.1875 to 0.1875
- w_up: bfloat16 [1024, 4608], P(None, 'tensor'), may hold values from -0.1875 to 0.1875
- w_down: bfloat16 [4608, 1024], P('tensor'), may hold values from -0.09375 to 0.09375
- gain_mix: float32 [1024], replicated, may hold values from 0.25 to 1.75
- gain_mlp: float32 [1024], replicated, may hold values from 0.25 to 1.75
- cotangent: bfloat16 [16384, 1024], P(('dp', 'tensor')), may hold values from -6 to 6
Outputs:
- result: float32 [16384, 1024], P(('dp', 'tensor'))
- grad_tokens: float32 [16384, 1024], P(('dp', 'tensor'))
- grad_w_in: float32 [1024, 3, 1024], P(None, None, 'tensor')
- grad_kernel: float32 [3, 1024], P(None, 'tensor')
- grad_w_out: float32 [1024, 1024], P('tensor')
- grad_w_gate: float32 [1024, 4608], P(None, 'tensor')
- grad_w_up: float32 [1024, 4608], P(None, 'tensor')
- grad_w_down: float32 [4608, 1024], P('tensor')
- grad_gain_mix: float32 [1024], replicated
- grad_gain_mlp: float32 [1024], replicated
The draws below stay inside these ranges and needn't reach their ends.
All inputs are finite; a program needn't handle non-finite values.
Results may differ from the reference program's by a relative error of at most 0.011.
Values may be sent and summed in bfloat16 or wider, within the bound.
A program may use at most 192 MiB of HBM per device.

```python
import jax
import jax.numpy as jnp
from jax import lax

D = 1024
FF = 4608
KERNEL = 3
LEN = 1024
SEQ_DEV = 2
TOKENS = 16384
N_DP = 8


def block_scale(own_key, extent, shards, low, largest):
    def one(axis_at, parts):
        heights = jax.random.uniform(jax.random.fold_in(jax.random.fold_in(own_key, 6), axis_at), (parts,), jnp.float32, low / len(shards), largest / len(shards))
        return jnp.repeat(jnp.exp(heights), extent[axis_at] // parts).reshape((-1,) + (1,) * (len(extent) - axis_at - 1))

    loudness = one(*shards[0])
    for cut in shards[1:]:
        loudness = loudness * one(*cut)
    return loudness


def centred(own_key, shape, scale, most, shards=(), dtype=jnp.bfloat16):
    result = scale * jax.random.normal(own_key, shape, jnp.float32)
    if shards:
        result = result * block_scale(own_key, shape, shards, -0.22, 0.18)
    return jnp.clip(result, -most, most).astype(dtype)


def setup_inputs(seed: int = 0) -> dict:
    splits = jax.random.split(jax.random.key(seed), 11)
    tokens = centred(splits[0], (TOKENS, D), 1.0, 6.0, ((0, 32),))
    w_in = centred(splits[1], (D, 3, D), D ** -0.5, 0.1875, ((2, 4),))
    conv_kernel = centred(splits[2], (KERNEL, D), KERNEL ** -0.5, 3.5, ((1, 4),))
    w_out = centred(splits[3], (D, D), D ** -0.5, 0.1875, ((0, 4),))
    w_gate = centred(splits[4], (D, FF), D ** -0.5, 0.1875, ((1, 4),))
    w_up = centred(splits[5], (D, FF), D ** -0.5, 0.1875, ((1, 4),))
    w_down = centred(splits[6], (FF, D), FF ** -0.5, 0.09375, ((0, 4),))
    gain_mix = jnp.clip(1.0 + 0.15 * jax.random.normal(splits[7], (D,), jnp.float32), 0.25, 1.75)
    gain_mlp = jnp.clip(1.0 + 0.15 * jax.random.normal(splits[8], (D,), jnp.float32), 0.25, 1.75)
    cotangent = centred(splits[9], (TOKENS, D), 1.0, 6.0, ((0, 32),))
    return {"tokens": tokens, "w_in": w_in, "conv_kernel": conv_kernel, "w_out": w_out, "w_gate": w_gate, "w_up": w_up, "w_down": w_down, "gain_mix": gain_mix, "gain_mlp": gain_mlp, "cotangent": cotangent}


EPSILON = 1e-05

@jax.custom_vjp
def low(v):
    return lax.optimization_barrier(v.astype(jnp.bfloat16)).astype(jnp.float32)

@jax.custom_vjp
def low_back(v):
    return v

def low_keep(v):
    return (low(v), None)

def low_pass(kept, grad):
    return (grad,)

def back_keep(v):
    return (v, None)

def back_low(kept, grad):
    return (low(grad),)
low.defvjp(low_keep, low_pass)
low_back.defvjp(back_keep, back_low)

def wide_dot(left, right):
    return jnp.dot(left, right, precision=lax.Precision.HIGHEST, preferred_element_type=jnp.float32)

def rms_unit(values):
    return values * lax.rsqrt(lax.optimization_barrier(jnp.mean(values * values, axis=-1, keepdims=True)) + EPSILON)

def causal_mix(values, kernel):
    back_one = jnp.pad(values, ((0, 0), (1, 0), (0, 0)))[:, :-1]
    back_two = jnp.pad(values, ((0, 0), (2, 0), (0, 0)))[:, :-2]
    return kernel[0] * back_two + kernel[1] * back_one + kernel[2] * values

def forward(inputs, w_in, conv_kernel, w_out, w_gate, w_up, w_down, gain_mix, gain_mlp):
    normed_one = low(rms_unit(inputs) * gain_mix)
    projected = low_back(wide_dot(normed_one, w_in.reshape(D, 3 * D)))
    b_part = projected[:, :D]
    c_part = projected[:, D:2 * D]
    x_part = projected[:, 2 * D:]
    gated = (b_part * x_part).reshape(-1, LEN, D)
    convolved = causal_mix(gated, conv_kernel).reshape(-1, D)
    mixed = low(c_part * convolved)
    resid = inputs + low_back(wide_dot(mixed, w_out))
    normed_two = low(rms_unit(resid) * gain_mlp)
    gate_pre = low_back(wide_dot(normed_two, w_gate))
    up_pre = low_back(wide_dot(normed_two, w_up))
    hidden = low(jax.nn.silu(gate_pre) * up_pre)
    return resid + low_back(wide_dot(hidden, w_down))

def reference(tokens, w_in, conv_kernel, w_out, w_gate, w_up, w_down, gain_mix, gain_mlp, cotangent):
    params = (w_in.astype(jnp.float32), conv_kernel.astype(jnp.float32), w_out.astype(jnp.float32), w_gate.astype(jnp.float32), w_up.astype(jnp.float32), w_down.astype(jnp.float32), gain_mix.astype(jnp.float32), gain_mlp.astype(jnp.float32))
    groups = tokens.astype(jnp.float32).reshape(N_DP, SEQ_DEV * LEN, D)
    grad_groups = cotangent.astype(jnp.float32).reshape(N_DP, SEQ_DEV * LEN, D)

    def one_group(totals, item):
        inputs, grad_out = item
        output, pull = jax.vjp(forward, inputs, *params)
        grads = pull(grad_out)
        totals = tuple((total + grad for total, grad in zip(totals, grads[1:])))
        return (totals, (output, grads[0]))
    start = tuple((jnp.zeros(p.shape, jnp.float32) for p in params))
    totals, (outputs, input_grads) = lax.scan(one_group, start, (groups, grad_groups))
    return (outputs.reshape(TOKENS, D), input_grads.reshape(TOKENS, D), totals[0], totals[1], totals[2], totals[3], totals[4], totals[5], totals[6], totals[7])
```

```python
import jax
import jax.numpy as jnp
from jax import lax
from jax.sharding import PartitionSpec as P

LEN = 1024


EPSILON = 1e-05


def rms_scale(values):
    scale = lax.rsqrt(jnp.mean(values * values, axis=-1, keepdims=True) + EPSILON)
    return (values * scale, scale)


def norm_back(grad_norm, unit, scale, gain):
    weighted = grad_norm * gain
    return scale * (weighted - unit * jnp.mean(weighted * unit, axis=-1, keepdims=True))


def shift_down(values, shift_by):
    return jnp.pad(values, ((0, 0), (shift_by, 0), (0, 0)))[:, : values.shape[1], :]


def shift_up(values, shift_by):
    return jnp.pad(values, ((0, 0), (0, shift_by), (0, 0)))[:, shift_by:, :]


def dot_first(left, right):
    return lax.dot_general(
        left, right, (((0,), (0,)), ((), ())), preferred_element_type=jnp.float32
    )


def dot_last(left, right):
    return lax.dot_general(
        left, right, (((1,), (1,)), ((), ())), preferred_element_type=jnp.float32
    )


def shards(tokens, w_in, conv_kernel, w_out, w_gate, w_up, w_down, gain_mix, gain_mlp, cotangent):
    model_width = tokens.shape[1]
    channels = conv_kernel.shape[1]
    in_flat = w_in.reshape(model_width, 3 * channels)
    taps = conv_kernel.astype(jnp.float32)
    inputs = tokens.astype(jnp.float32)
    unit_one, scale_one = rms_scale(inputs)
    normed_one = lax.all_gather(
        (unit_one * gain_mix).astype(jnp.bfloat16), "tensor", axis=0, tiled=True
    )
    projected = jnp.dot(normed_one, in_flat, preferred_element_type=jnp.float32)
    b_part = projected[:, :channels]
    c_part = projected[:, channels : 2 * channels]
    x_part = projected[:, 2 * channels :]
    seq_gated = (b_part * x_part).reshape(-1, LEN, channels)
    back_one = shift_down(seq_gated, 1)
    back_two = shift_down(seq_gated, 2)
    convolved = (taps[0] * back_two + taps[1] * back_one + taps[2] * seq_gated).reshape(
        -1, channels
    )
    mixed_low = (c_part * convolved).astype(jnp.bfloat16)
    resid = inputs + lax.psum_scatter(
        jnp.dot(mixed_low, w_out, preferred_element_type=jnp.float32),
        "tensor",
        scatter_dimension=0,
        tiled=True,
    )
    unit_two, scale_two = rms_scale(resid)
    normed_two = lax.all_gather(
        (unit_two * gain_mlp).astype(jnp.bfloat16), "tensor", axis=0, tiled=True
    )
    gate_pre = jnp.dot(normed_two, w_gate, preferred_element_type=jnp.float32)
    up_pre = jnp.dot(normed_two, w_up, preferred_element_type=jnp.float32)
    sig_gate = jax.nn.sigmoid(gate_pre)
    activated = gate_pre * sig_gate
    hidden_low = (activated * up_pre).astype(jnp.bfloat16)
    result = resid + lax.psum_scatter(
        jnp.dot(hidden_low, w_down, preferred_element_type=jnp.float32).astype(jnp.bfloat16),
        "tensor",
        scatter_dimension=0,
        tiled=True,
    ).astype(jnp.float32)
    grad_full = lax.all_gather(cotangent, "tensor", axis=0, tiled=True)
    grad_down = dot_first(hidden_low, grad_full)
    grad_hidden = dot_last(grad_full, w_down)
    grad_gate_low = (grad_hidden * up_pre * sig_gate * (1.0 + gate_pre * (1.0 - sig_gate))).astype(
        jnp.bfloat16
    )
    grad_up_low = (grad_hidden * activated).astype(jnp.bfloat16)
    grad_wgate = dot_first(normed_two, grad_gate_low)
    grad_wup = dot_first(normed_two, grad_up_low)
    back_rows = lax.psum_scatter(
        dot_last(grad_gate_low, w_gate) + dot_last(grad_up_low, w_up),
        "tensor",
        scatter_dimension=0,
        tiled=True,
    )
    grad_resid = cotangent.astype(jnp.float32) + norm_back(back_rows, unit_two, scale_two, gain_mlp)
    grad_gain_two = jnp.sum(back_rows * unit_two, axis=0)
    grad_mixed = lax.all_gather(grad_resid.astype(jnp.bfloat16), "tensor", axis=0, tiled=True)
    grad_wout = dot_first(mixed_low, grad_mixed)
    grad_conv_out = dot_last(grad_mixed, w_out)
    grad_c = grad_conv_out * convolved
    seq_grad = (grad_conv_out * c_part).reshape(-1, LEN, channels)
    grad_gated = (
        taps[0] * shift_up(seq_grad, 2) + taps[1] * shift_up(seq_grad, 1) + taps[2] * seq_grad
    ).reshape(-1, channels)
    grad_taps = jnp.stack(
        [
            jnp.sum(seq_grad * back_two, axis=(0, 1)),
            jnp.sum(seq_grad * back_one, axis=(0, 1)),
            jnp.sum(seq_grad * seq_gated, axis=(0, 1)),
        ]
    )
    grad_proj_low = jnp.concatenate(
        [grad_gated * x_part, grad_c, grad_gated * b_part], axis=1
    ).astype(jnp.bfloat16)
    grad_win = dot_first(normed_one, grad_proj_low).reshape(model_width, 3, channels)
    back_first = lax.psum_scatter(
        dot_last(grad_proj_low, in_flat), "tensor", scatter_dimension=0, tiled=True
    )
    grad_gain_one = jnp.sum(back_first * unit_one, axis=0)
    grad_tokens = grad_resid + norm_back(back_first, unit_one, scale_one, gain_mix)
    grad_win, grad_taps, grad_wout, grad_wgate, grad_wup, grad_down = lax.psum(
        (grad_win, grad_taps, grad_wout, grad_wgate, grad_wup, grad_down), "dp"
    )
    grad_gain_one, grad_gain_two = lax.psum((grad_gain_one, grad_gain_two), ("dp", "tensor"))
    return (
        result,
        grad_tokens,
        grad_win,
        grad_taps,
        grad_wout,
        grad_wgate,
        grad_wup,
        grad_down,
        grad_gain_one,
        grad_gain_two,
    )


def swap(values, axis, step):
    count = lax.axis_size(axis)
    return lax.ppermute(values, axis, [(i, i ^ step) for i in range(count)])


def part(values, index):
    size = values.shape[0] // 2
    return lax.dynamic_slice_in_dim(values, index * size, size, axis=0)


def in_order(bit, mine, other):
    return jnp.concatenate(
        [jnp.where(bit == 0, mine, other), jnp.where(bit == 0, other, mine)], axis=0
    )


def halving(values, order):
    place = lax.axis_index("dp")
    piece = values.astype(jnp.bfloat16)
    for step in order:
        bit = (place // step) % 2
        arrived = swap(part(piece, 1 - bit), "dp", step)
        piece = (
            part(piece, bit).astype(jnp.float32) + arrived.astype(jnp.float32)
        ).astype(jnp.bfloat16)
    for step in reversed(order):
        bit = (place // step) % 2
        piece = in_order(bit, piece, swap(piece, "dp", step))
    return piece


def dp_sum(values):
    rows = values.shape[0]
    cut = max(rows * 5 // 8 // 128, 1) * 128
    return jnp.concatenate(
        [halving(values[:cut], (1, 2, 4)), halving(values[cut:], (2, 1, 4))], axis=0
    ).astype(jnp.float32)


def small_sum(values, axis):
    step = 1
    while step < lax.axis_size(axis):
        values = values + swap(values, axis, step)
        step *= 2
    return values


def gather_pair(own, core, after=None):
    near = in_order(core, own, swap(own, "tensor", 1))
    if after is not None:
        own, _ = lax.optimization_barrier((own, after))
    across = swap(own, "tensor", 2)
    far = in_order(core, across, swap(across, "tensor", 1))
    return near, far, across


def reduce_far(far, core):
    low = jnp.bfloat16
    arrived = swap(part(far, 1 - core), "tensor", 1)
    total = (part(far, core).astype(jnp.float32) + arrived.astype(jnp.float32)).astype(low)
    return swap(total, "tensor", 2)


def reduce_near(near, core, crossed):
    arrived = swap(part(near, 1 - core), "tensor", 1)
    return (
        part(near, core).astype(jnp.float32)
        + arrived.astype(jnp.float32)
        + crossed.astype(jnp.float32)
    )


def dot(left, right):
    return jnp.dot(left, right, preferred_element_type=jnp.float32)


def down(values, shift_by):
    return jnp.pad(values, ((shift_by, 0), (0, 0)))[: values.shape[0]]


def up(values, shift_by):
    return jnp.pad(values, ((0, shift_by), (0, 0)))[shift_by:]


def conv_forward(normed, in_flat, taps):
    channels = taps.shape[1]
    projected = dot(normed, in_flat)
    b_part = projected[:, :channels]
    c_part = projected[:, channels : 2 * channels]
    x_part = projected[:, 2 * channels :]
    gated = b_part * x_part
    convolved = taps[0] * down(gated, 2) + taps[1] * down(gated, 1) + taps[2] * gated
    mixed = (c_part * convolved).astype(jnp.bfloat16)
    return mixed, (b_part, c_part, x_part, gated, convolved)


def conv_backward(grad_mixed, kept, w_out, taps):
    b_part, c_part, x_part, gated, convolved = kept
    grad_conv_out = dot_last(grad_mixed, w_out)
    grad_c = grad_conv_out * convolved
    grad_conv = grad_conv_out * c_part
    grad_gated = taps[0] * up(grad_conv, 2) + taps[1] * up(grad_conv, 1) + taps[2] * grad_conv
    grad_taps = jnp.stack(
        [
            jnp.sum(grad_conv * down(gated, 2), axis=0),
            jnp.sum(grad_conv * down(gated, 1), axis=0),
            jnp.sum(grad_conv * gated, axis=0),
        ]
    )
    grad_projected = jnp.concatenate(
        [grad_gated * x_part, grad_c, grad_gated * b_part], axis=1
    ).astype(jnp.bfloat16)
    return grad_projected, grad_taps


def mlp_forward(normed, w_gate, w_up):
    gate_pre = dot(normed, w_gate)
    up_pre = dot(normed, w_up)
    sig_gate = jax.nn.sigmoid(gate_pre)
    hidden = (gate_pre * sig_gate * up_pre).astype(jnp.bfloat16)
    return hidden, (gate_pre, up_pre, sig_gate)


def mlp_backward(grad_out, kept, w_gate, w_up, w_down):
    gate_pre, up_pre, sig_gate = kept
    grad_hidden = dot_last(grad_out, w_down)
    grad_gate = (grad_hidden * up_pre * sig_gate * (1.0 + gate_pre * (1.0 - sig_gate))).astype(
        jnp.bfloat16
    )
    grad_up = (grad_hidden * gate_pre * sig_gate).astype(jnp.bfloat16)
    back = (dot_last(grad_gate, w_gate) + dot_last(grad_up, w_up)).astype(jnp.bfloat16)
    return grad_gate, grad_up, back


def pair_shards(
    tokens, w_in, conv_kernel, w_out, w_gate, w_up, w_down, gain_mix, gain_mlp, cotangent
):
    low = jnp.bfloat16
    model_width = tokens.shape[1]
    channels = conv_kernel.shape[1]
    core = lax.axis_index("tensor") % 2
    in_flat = w_in.reshape(model_width, 3 * channels)
    taps = conv_kernel.astype(jnp.float32)
    inputs = tokens.astype(jnp.float32)
    unit_one, scale_one = rms_scale(inputs)
    one_near, one_far, _ = gather_pair((unit_one * gain_mix).astype(low), core)
    mixed_near, kept_near = conv_forward(one_near, in_flat, taps)
    mixed_far, kept_far = conv_forward(one_far, in_flat, taps)
    crossed = reduce_far(dot(mixed_far, w_out).astype(low), core)
    resid = inputs + reduce_near(dot(mixed_near, w_out).astype(low), core, crossed)
    unit_two, scale_two = rms_scale(resid)
    two_near, two_far, two_across = gather_pair((unit_two * gain_mlp).astype(low), core)
    cot_near, cot_far, _ = gather_pair(cotangent, core, after=two_across)
    hidden_near, mlp_near = mlp_forward(two_near, w_gate, w_up)
    gate_near, up_near, back_near = mlp_backward(cot_near, mlp_near, w_gate, w_up, w_down)
    hidden_far, mlp_far = mlp_forward(two_far, w_gate, w_up)
    out_crossed = reduce_far(dot(hidden_far, w_down).astype(low), core)
    gate_far, up_far, back_far = mlp_backward(cot_far, mlp_far, w_gate, w_up, w_down)
    back_crossed = reduce_far(back_far, core)
    grad_down = dp_sum(dot_first(hidden_near, cot_near) + dot_first(hidden_far, cot_far))
    grad_wgate = dp_sum(dot_first(two_near, gate_near) + dot_first(two_far, gate_far))
    grad_wup = dp_sum(dot_first(two_near, up_near) + dot_first(two_far, up_far))
    result = resid + reduce_near(dot(hidden_near, w_down).astype(low), core, out_crossed)
    back_rows = reduce_near(back_near, core, back_crossed)
    grad_resid = cotangent.astype(jnp.float32) + norm_back(back_rows, unit_two, scale_two, gain_mlp)
    gain_two = jnp.sum(back_rows * unit_two, axis=0)
    gm_near, gm_far, _ = gather_pair(grad_resid.astype(low), core)
    gp_near, taps_near = conv_backward(gm_near, kept_near, w_out, taps)
    gp_far, taps_far = conv_backward(gm_far, kept_far, w_out, taps)
    first_crossed = reduce_far(dot_last(gp_far, in_flat).astype(low), core)
    grad_wout = dp_sum(dot_first(mixed_near, gm_near) + dot_first(mixed_far, gm_far))
    grad_win = dp_sum(dot_first(one_near, gp_near) + dot_first(one_far, gp_far))
    back_first = reduce_near(dot_last(gp_near, in_flat).astype(low), core, first_crossed)
    gain_one = jnp.sum(back_first * unit_one, axis=0)
    grad_tokens = grad_resid + norm_back(back_first, unit_one, scale_one, gain_mix)
    gains = small_sum(jnp.stack([gain_one, gain_two]), "tensor")
    small = small_sum(
        jnp.concatenate([gains.reshape(-1), (taps_near + taps_far).reshape(-1)]), "dp"
    )
    return (
        result,
        grad_tokens,
        grad_win.reshape(model_width, 3, channels),
        small[2 * model_width :].reshape(3, channels),
        grad_wout,
        grad_wgate,
        grad_wup,
        grad_down,
        small[:model_width],
        small[model_width : 2 * model_width],
    )


def solution(mesh):
    placed = (
        P(("dp", "tensor"), None),
        P(None, None, "tensor"),
        P(None, "tensor"),
        P("tensor", None),
        P(None, "tensor"),
        P(None, "tensor"),
        P("tensor", None),
        P(),
        P(),
        P(("dp", "tensor"), None),
    )
    paired = mesh.shape["tensor"] == 4 and mesh.shape["dp"] == 8
    return jax.shard_map(
        pair_shards if paired else shards,
        mesh=mesh,
        in_specs=placed,
        out_specs=(
            P(("dp", "tensor"), None),
            P(("dp", "tensor"), None),
            P(None, None, "tensor"),
            P(None, "tensor"),
            P("tensor", None),
            P(None, "tensor"),
            P(None, "tensor"),
            P("tensor", None),
            P(),
            P(),
        ),
        check_vma=False,
    )
```

```python
import jax
import jax.numpy as jnp
from jax import lax
from jax.sharding import PartitionSpec as P

LEN = 1024


EPSILON = 1e-05


def rms_scale(values):
    scale = lax.rsqrt(jnp.mean(values * values, axis=-1, keepdims=True) + EPSILON)
    return (values * scale, scale)


def norm_back(grad_norm, unit, scale, gain):
    weighted = grad_norm * gain
    return scale * (weighted - unit * jnp.mean(weighted * unit, axis=-1, keepdims=True))


def shift_down(values, shift_by):
    return jnp.pad(values, ((0, 0), (shift_by, 0), (0, 0)))[:, : values.shape[1], :]


def shift_up(values, shift_by):
    return jnp.pad(values, ((0, 0), (0, shift_by), (0, 0)))[:, shift_by:, :]


def dot_first(left, right):
    return lax.dot_general(
        left, right, (((0,), (0,)), ((), ())), preferred_element_type=jnp.float32
    )


def dot_last(left, right):
    return lax.dot_general(
        left, right, (((1,), (1,)), ((), ())), preferred_element_type=jnp.float32
    )


def shards(tokens, w_in, conv_kernel, w_out, w_gate, w_up, w_down, gain_mix, gain_mlp, cotangent):
    model_width = tokens.shape[1]
    channels = conv_kernel.shape[1]
    in_flat = w_in.reshape(model_width, 3 * channels)
    taps = conv_kernel.astype(jnp.float32)
    inputs = tokens.astype(jnp.float32)
    unit_one, scale_one = rms_scale(inputs)
    normed_one = lax.all_gather(
        (unit_one * gain_mix).astype(jnp.bfloat16), "tensor", axis=0, tiled=True
    )
    projected = jnp.dot(normed_one, in_flat, preferred_element_type=jnp.float32)
    b_part = projected[:, :channels]
    c_part = projected[:, channels : 2 * channels]
    x_part = projected[:, 2 * channels :]
    seq_gated = (b_part * x_part).reshape(-1, LEN, channels)
    back_one = shift_down(seq_gated, 1)
    back_two = shift_down(seq_gated, 2)
    convolved = (taps[0] * back_two + taps[1] * back_one + taps[2] * seq_gated).reshape(
        -1, channels
    )
    mixed_low = (c_part * convolved).astype(jnp.bfloat16)
    resid = inputs + lax.psum_scatter(
        jnp.dot(mixed_low, w_out, preferred_element_type=jnp.float32),
        "tensor",
        scatter_dimension=0,
        tiled=True,
    )
    unit_two, scale_two = rms_scale(resid)
    normed_two = lax.all_gather(
        (unit_two * gain_mlp).astype(jnp.bfloat16), "tensor", axis=0, tiled=True
    )
    gate_pre = jnp.dot(normed_two, w_gate, preferred_element_type=jnp.float32)
    up_pre = jnp.dot(normed_two, w_up, preferred_element_type=jnp.float32)
    sig_gate = jax.nn.sigmoid(gate_pre)
    activated = gate_pre * sig_gate
    hidden_low = (activated * up_pre).astype(jnp.bfloat16)
    result = resid + lax.psum_scatter(
        jnp.dot(hidden_low, w_down, preferred_element_type=jnp.float32).astype(jnp.bfloat16),
        "tensor",
        scatter_dimension=0,
        tiled=True,
    ).astype(jnp.float32)
    grad_full = lax.all_gather(cotangent, "tensor", axis=0, tiled=True)
    grad_down = dot_first(hidden_low, grad_full)
    grad_hidden = dot_last(grad_full, w_down)
    grad_gate_low = (grad_hidden * up_pre * sig_gate * (1.0 + gate_pre * (1.0 - sig_gate))).astype(
        jnp.bfloat16
    )
    grad_up_low = (grad_hidden * activated).astype(jnp.bfloat16)
    grad_wgate = dot_first(normed_two, grad_gate_low)
    grad_wup = dot_first(normed_two, grad_up_low)
    back_rows = lax.psum_scatter(
        dot_last(grad_gate_low, w_gate) + dot_last(grad_up_low, w_up),
        "tensor",
        scatter_dimension=0,
        tiled=True,
    )
    grad_resid = cotangent.astype(jnp.float32) + norm_back(back_rows, unit_two, scale_two, gain_mlp)
    grad_gain_two = jnp.sum(back_rows * unit_two, axis=0)
    grad_mixed = lax.all_gather(grad_resid.astype(jnp.bfloat16), "tensor", axis=0, tiled=True)
    grad_wout = dot_first(mixed_low, grad_mixed)
    grad_conv_out = dot_last(grad_mixed, w_out)
    grad_c = grad_conv_out * convolved
    seq_grad = (grad_conv_out * c_part).reshape(-1, LEN, channels)
    grad_gated = (
        taps[0] * shift_up(seq_grad, 2) + taps[1] * shift_up(seq_grad, 1) + taps[2] * seq_grad
    ).reshape(-1, channels)
    grad_taps = jnp.stack(
        [
            jnp.sum(seq_grad * back_two, axis=(0, 1)),
            jnp.sum(seq_grad * back_one, axis=(0, 1)),
            jnp.sum(seq_grad * seq_gated, axis=(0, 1)),
        ]
    )
    grad_proj_low = jnp.concatenate(
        [grad_gated * x_part, grad_c, grad_gated * b_part], axis=1
    ).astype(jnp.bfloat16)
    grad_win = dot_first(normed_one, grad_proj_low).reshape(model_width, 3, channels)
    back_first = lax.psum_scatter(
        dot_last(grad_proj_low, in_flat), "tensor", scatter_dimension=0, tiled=True
    )
    grad_gain_one = jnp.sum(back_first * unit_one, axis=0)
    grad_tokens = grad_resid + norm_back(back_first, unit_one, scale_one, gain_mix)
    grad_win, grad_taps, grad_wout, grad_wgate, grad_wup, grad_down = lax.psum(
        (grad_win, grad_taps, grad_wout, grad_wgate, grad_wup, grad_down), "dp"
    )
    grad_gain_one, grad_gain_two = lax.psum((grad_gain_one, grad_gain_two), ("dp", "tensor"))
    return (
        result,
        grad_tokens,
        grad_win,
        grad_taps,
        grad_wout,
        grad_wgate,
        grad_wup,
        grad_down,
        grad_gain_one,
        grad_gain_two,
    )


def swap(values, axis, step):
    count = lax.axis_size(axis)
    return lax.ppermute(values, axis, [(i, i ^ step) for i in range(count)])


def part(values, index):
    size = values.shape[0] // 2
    return lax.dynamic_slice_in_dim(values, index * size, size, axis=0)


def in_order(bit, mine, other):
    return jnp.concatenate(
        [jnp.where(bit == 0, mine, other), jnp.where(bit == 0, other, mine)], axis=0
    )


def tied(values, after):
    return lax.optimization_barrier((values, after))[0]


class Sum:
    def __init__(self, values):
        rows = values.shape[0]
        cut = max(rows * 5 // 8 // 128, 1) * 128
        low = values.astype(jnp.bfloat16)
        self.place = lax.axis_index("dp")
        self.pieces = [low[:cut], low[cut:]]
        self.sent = None
        self.stage = 0
        self.start()

    def bit(self, step):
        return (self.place // step) % 2

    def steps(self):
        return {0: (1, 2), 1: (2, 1), 2: (4,), 3: (4,), 4: (2, 1), 5: (1, 2)}[self.stage]

    def start(self):
        steps = self.steps()
        if self.stage == 2:
            self.pieces = [jnp.concatenate(self.pieces, axis=0)]
        out = self.pieces
        if self.stage < 3:
            out = [part(p, 1 - self.bit(step)) for p, step in zip(out, steps)]
        self.sent = [swap(p, "dp", step) for p, step in zip(out, steps)]

    def advance(self, after=None):
        steps = self.steps()
        arrived = self.sent
        if after is not None:
            arrived = tied(arrived, after)
        if self.stage < 3:
            self.pieces = [
                (
                    part(p, self.bit(step)).astype(jnp.float32) + got.astype(jnp.float32)
                ).astype(jnp.bfloat16)
                for p, got, step in zip(self.pieces, arrived, steps)
            ]
        else:
            self.pieces = [
                in_order(self.bit(step), p, got)
                for p, got, step in zip(self.pieces, arrived, steps)
            ]
        if self.stage == 2:
            self.cut = self.sizes[0]
        if self.stage == 3:
            whole = self.pieces[0]
            self.pieces = [whole[: self.cut], whole[self.cut :]]
        if self.stage == 1:
            self.sizes = [p.shape[0] for p in self.pieces]
        self.stage += 1
        if self.stage < 6:
            self.start()

    def finish(self):
        while self.stage < 6:
            self.advance()
        return jnp.concatenate(self.pieces, axis=0).astype(jnp.float32)


def small_sum(values, axis):
    step = 1
    while step < lax.axis_size(axis):
        values = values + swap(values, axis, step)
        step *= 2
    return values


def gather_pair(own, core, after=None):
    near = in_order(core, own, swap(own, "tensor", 1))
    if after is not None:
        own, _ = lax.optimization_barrier((own, after))
    across = swap(own, "tensor", 2)
    far = in_order(core, across, swap(across, "tensor", 1))
    return near, far, across


def sum_far(far, core):
    arrived = swap(part(far, 1 - core), "tensor", 1)
    return (part(far, core).astype(jnp.float32) + arrived.astype(jnp.float32)).astype(jnp.bfloat16)


def reduce_far(far, core):
    return swap(sum_far(far, core), "tensor", 2)


def reduce_near(near, core, crossed):
    arrived = swap(part(near, 1 - core), "tensor", 1)
    return (
        part(near, core).astype(jnp.float32)
        + arrived.astype(jnp.float32)
        + crossed.astype(jnp.float32)
    )


def dot(left, right):
    return jnp.dot(left, right, preferred_element_type=jnp.float32)


def down(values, shift_by):
    return jnp.pad(values, ((shift_by, 0), (0, 0)))[: values.shape[0]]


def up(values, shift_by):
    return jnp.pad(values, ((0, shift_by), (0, 0)))[shift_by:]


def conv_forward(normed, in_flat, taps):
    channels = taps.shape[1]
    projected = dot(normed, in_flat)
    b_part = projected[:, :channels]
    c_part = projected[:, channels : 2 * channels]
    x_part = projected[:, 2 * channels :]
    gated = b_part * x_part
    convolved = taps[0] * down(gated, 2) + taps[1] * down(gated, 1) + taps[2] * gated
    mixed = (c_part * convolved).astype(jnp.bfloat16)
    return mixed, (b_part, c_part, x_part, gated, convolved)


def conv_backward(grad_mixed, kept, w_out, taps):
    b_part, c_part, x_part, gated, convolved = kept
    grad_conv_out = dot_last(grad_mixed, w_out)
    grad_c = grad_conv_out * convolved
    grad_conv = grad_conv_out * c_part
    grad_gated = taps[0] * up(grad_conv, 2) + taps[1] * up(grad_conv, 1) + taps[2] * grad_conv
    grad_taps = jnp.stack(
        [
            jnp.sum(grad_conv * down(gated, 2), axis=0),
            jnp.sum(grad_conv * down(gated, 1), axis=0),
            jnp.sum(grad_conv * gated, axis=0),
        ]
    )
    grad_projected = jnp.concatenate(
        [grad_gated * x_part, grad_c, grad_gated * b_part], axis=1
    ).astype(jnp.bfloat16)
    return grad_projected, grad_taps


def mlp_forward(normed, w_gate, w_up):
    gate_pre = dot(normed, w_gate)
    up_pre = dot(normed, w_up)
    sig_gate = jax.nn.sigmoid(gate_pre)
    hidden = (gate_pre * sig_gate * up_pre).astype(jnp.bfloat16)
    return hidden, (gate_pre, up_pre, sig_gate)


def mlp_backward(grad_out, kept, w_gate, w_up, w_down):
    gate_pre, up_pre, sig_gate = kept
    grad_hidden = dot_last(grad_out, w_down)
    grad_gate = (grad_hidden * up_pre * sig_gate * (1.0 + gate_pre * (1.0 - sig_gate))).astype(
        jnp.bfloat16
    )
    grad_up = (grad_hidden * gate_pre * sig_gate).astype(jnp.bfloat16)
    back = (dot_last(grad_gate, w_gate) + dot_last(grad_up, w_up)).astype(jnp.bfloat16)
    return grad_gate, grad_up, back


def pair_shards(
    tokens, w_in, conv_kernel, w_out, w_gate, w_up, w_down, gain_mix, gain_mlp, cotangent
):
    low = jnp.bfloat16
    model_width = tokens.shape[1]
    channels = conv_kernel.shape[1]
    core = lax.axis_index("tensor") % 2
    in_flat = w_in.reshape(model_width, 3 * channels)
    taps = conv_kernel.astype(jnp.float32)
    inputs = tokens.astype(jnp.float32)
    unit_one, scale_one = rms_scale(inputs)
    one_near, one_far, _ = gather_pair((unit_one * gain_mix).astype(low), core)
    mixed_near, kept_near = conv_forward(one_near, in_flat, taps)
    mixed_far, kept_far = conv_forward(one_far, in_flat, taps)
    crossed = reduce_far(dot(mixed_far, w_out).astype(low), core)
    resid = inputs + reduce_near(dot(mixed_near, w_out).astype(low), core, crossed)
    unit_two, scale_two = rms_scale(resid)
    two_near, two_far, two_across = gather_pair((unit_two * gain_mlp).astype(low), core)
    cot_near, cot_far, _ = gather_pair(cotangent, core, after=two_across)
    hidden_near, mlp_near = mlp_forward(two_near, w_gate, w_up)
    gate_near, up_near, back_near = mlp_backward(cot_near, mlp_near, w_gate, w_up, w_down)
    hidden_far, mlp_far = mlp_forward(tied(two_far, back_near), w_gate, w_up)
    grad_down = (dot_first(hidden_near, cot_near) + dot_first(hidden_far, cot_far)).astype(low)
    sum_down = Sum(grad_down)
    gate_far, up_far, back_far = mlp_backward(
        tied(cot_far, grad_down), mlp_far, w_gate, w_up, w_down
    )
    back_sum = sum_far(back_far, core)
    back_crossed = swap(back_sum, "tensor", 2)
    sum_down.advance(after=back_sum)
    grad_gate = (dot_first(two_near, gate_near) + dot_first(two_far, gate_far)).astype(low)
    sum_gate = Sum(grad_gate)
    grad_up = (dot_first(two_near, up_near) + dot_first(two_far, up_far)).astype(low)
    sum_up = Sum(grad_up)
    back_rows = reduce_near(back_near, core, tied(back_crossed, grad_up))
    grad_resid = cotangent.astype(jnp.float32) + norm_back(back_rows, unit_two, scale_two, gain_mlp)
    gain_two = jnp.sum(back_rows * unit_two, axis=0)
    grad_mixed = grad_resid.astype(low)
    gm_near, gm_far, _ = gather_pair(grad_mixed, core)
    sum_down.advance(after=grad_mixed)
    sum_gate.advance(after=grad_mixed)
    out_crossed = reduce_far(dot(hidden_far, w_down).astype(low), core)
    gp_near, taps_near = conv_backward(gm_near, kept_near, w_out, taps)
    first_near = dot_last(gp_near, in_flat).astype(low)
    sum_down.advance(after=first_near)
    sum_up.advance(after=first_near)
    gp_far, taps_far = conv_backward(gm_far, kept_far, w_out, taps)
    first_sum = sum_far(dot_last(gp_far, in_flat).astype(low), core)
    first_crossed = swap(first_sum, "tensor", 2)
    grad_conv = jnp.concatenate(
        [
            dot_first(one_near, gp_near) + dot_first(one_far, gp_far),
            dot_first(gm_near, mixed_near) + dot_first(gm_far, mixed_far),
        ],
        axis=1,
    ).astype(low)
    sum_conv = Sum(grad_conv)
    sum_gate.advance(after=first_sum)
    sum_down.advance(after=first_sum)
    sum_up.advance(after=grad_conv)
    result = resid + reduce_near(dot(hidden_near, w_down).astype(low), core, out_crossed)
    back_first = reduce_near(first_near, core, first_crossed)
    gain_one = jnp.sum(back_first * unit_one, axis=0)
    grad_tokens = grad_resid + norm_back(back_first, unit_one, scale_one, gain_mix)
    gains = small_sum(jnp.stack([gain_one, gain_two]), "tensor")
    small = small_sum(
        jnp.concatenate([gains.reshape(-1), (taps_near + taps_far).reshape(-1)]), "dp"
    )
    sum_conv.advance()
    sum_down.advance(after=sum_conv.pieces[0])
    sum_gate.advance(after=sum_conv.pieces[0])
    sum_up.advance(after=sum_conv.pieces[0])
    sum_conv.advance()
    sum_gate.advance(after=sum_conv.pieces[0])
    sum_up.advance(after=sum_conv.pieces[0])
    grad_down = sum_down.finish()
    sum_conv.advance()
    sum_gate.advance(after=sum_conv.pieces[0])
    sum_up.advance(after=sum_conv.pieces[0])
    grad_wgate = sum_gate.finish()
    grad_wup = sum_up.finish()
    grad_conv = sum_conv.finish()
    grad_win = grad_conv[:, : 3 * channels]
    grad_wout = grad_conv[:, 3 * channels :].T
    return (
        result,
        grad_tokens,
        grad_win.reshape(model_width, 3, channels),
        small[2 * model_width :].reshape(3, channels),
        grad_wout,
        grad_wgate,
        grad_wup,
        grad_down,
        small[:model_width],
        small[model_width : 2 * model_width],
    )


def solution(mesh):
    placed = (
        P(("dp", "tensor"), None),
        P(None, None, "tensor"),
        P(None, "tensor"),
        P("tensor", None),
        P(None, "tensor"),
        P(None, "tensor"),
        P("tensor", None),
        P(),
        P(),
        P(("dp", "tensor"), None),
    )
    paired = mesh.shape["tensor"] == 4 and mesh.shape["dp"] == 8
    return jax.shard_map(
        pair_shards if paired else shards,
        mesh=mesh,
        in_specs=placed,
        out_specs=(
            P(("dp", "tensor"), None),
            P(("dp", "tensor"), None),
            P(None, None, "tensor"),
            P(None, "tensor"),
            P("tensor", None),
            P(None, "tensor"),
            P(None, "tensor"),
            P("tensor", None),
            P(),
            P(),
        ),
        check_vma=False,
    )
```

```python
import jax
import jax.numpy as jnp
from jax import lax
from jax.sharding import PartitionSpec as P

LEN = 1024


EPSILON = 1e-05


def rms_scale(values):
    scale = lax.rsqrt(jnp.mean(values * values, axis=-1, keepdims=True) + EPSILON)
    return (values * scale, scale)


def norm_back(grad_norm, unit, scale, gain):
    weighted = grad_norm * gain
    return scale * (weighted - unit * jnp.mean(weighted * unit, axis=-1, keepdims=True))


def shift_down(values, shift_by):
    return jnp.pad(values, ((0, 0), (shift_by, 0), (0, 0)))[:, : values.shape[1], :]


def shift_up(values, shift_by):
    return jnp.pad(values, ((0, 0), (0, shift_by), (0, 0)))[:, shift_by:, :]


def dot_first(left, right):
    return lax.dot_general(
        left, right, (((0,), (0,)), ((), ())), preferred_element_type=jnp.float32
    )


def dot_last(left, right):
    return lax.dot_general(
        left, right, (((1,), (1,)), ((), ())), preferred_element_type=jnp.float32
    )


def shards(tokens, w_in, conv_kernel, w_out, w_gate, w_up, w_down, gain_mix, gain_mlp, cotangent):
    model_width = tokens.shape[1]
    channels = conv_kernel.shape[1]
    in_flat = w_in.reshape(model_width, 3 * channels)
    taps = conv_kernel.astype(jnp.float32)
    inputs = tokens.astype(jnp.float32)
    unit_one, scale_one = rms_scale(inputs)
    normed_one = lax.all_gather(
        (unit_one * gain_mix).astype(jnp.bfloat16), "tensor", axis=0, tiled=True
    )
    projected = jnp.dot(normed_one, in_flat, preferred_element_type=jnp.float32)
    b_part = projected[:, :channels]
    c_part = projected[:, channels : 2 * channels]
    x_part = projected[:, 2 * channels :]
    seq_gated = (b_part * x_part).reshape(-1, LEN, channels)
    back_one = shift_down(seq_gated, 1)
    back_two = shift_down(seq_gated, 2)
    convolved = (taps[0] * back_two + taps[1] * back_one + taps[2] * seq_gated).reshape(
        -1, channels
    )
    mixed_low = (c_part * convolved).astype(jnp.bfloat16)
    resid = inputs + lax.psum_scatter(
        jnp.dot(mixed_low, w_out, preferred_element_type=jnp.float32),
        "tensor",
        scatter_dimension=0,
        tiled=True,
    )
    unit_two, scale_two = rms_scale(resid)
    normed_two = lax.all_gather(
        (unit_two * gain_mlp).astype(jnp.bfloat16), "tensor", axis=0, tiled=True
    )
    gate_pre = jnp.dot(normed_two, w_gate, preferred_element_type=jnp.float32)
    up_pre = jnp.dot(normed_two, w_up, preferred_element_type=jnp.float32)
    sig_gate = jax.nn.sigmoid(gate_pre)
    activated = gate_pre * sig_gate
    hidden_low = (activated * up_pre).astype(jnp.bfloat16)
    result = resid + lax.psum_scatter(
        jnp.dot(hidden_low, w_down, preferred_element_type=jnp.float32).astype(jnp.bfloat16),
        "tensor",
        scatter_dimension=0,
        tiled=True,
    ).astype(jnp.float32)
    grad_full = lax.all_gather(cotangent, "tensor", axis=0, tiled=True)
    grad_down = dot_first(hidden_low, grad_full)
    grad_hidden = dot_last(grad_full, w_down)
    grad_gate_low = (grad_hidden * up_pre * sig_gate * (1.0 + gate_pre * (1.0 - sig_gate))).astype(
        jnp.bfloat16
    )
    grad_up_low = (grad_hidden * activated).astype(jnp.bfloat16)
    grad_wgate = dot_first(normed_two, grad_gate_low)
    grad_wup = dot_first(normed_two, grad_up_low)
    back_rows = lax.psum_scatter(
        dot_last(grad_gate_low, w_gate) + dot_last(grad_up_low, w_up),
        "tensor",
        scatter_dimension=0,
        tiled=True,
    )
    grad_resid = cotangent.astype(jnp.float32) + norm_back(back_rows, unit_two, scale_two, gain_mlp)
    grad_gain_two = jnp.sum(back_rows * unit_two, axis=0)
    grad_mixed = lax.all_gather(grad_resid.astype(jnp.bfloat16), "tensor", axis=0, tiled=True)
    grad_wout = dot_first(mixed_low, grad_mixed)
    grad_conv_out = dot_last(grad_mixed, w_out)
    grad_c = grad_conv_out * convolved
    seq_grad = (grad_conv_out * c_part).reshape(-1, LEN, channels)
    grad_gated = (
        taps[0] * shift_up(seq_grad, 2) + taps[1] * shift_up(seq_grad, 1) + taps[2] * seq_grad
    ).reshape(-1, channels)
    grad_taps = jnp.stack(
        [
            jnp.sum(seq_grad * back_two, axis=(0, 1)),
            jnp.sum(seq_grad * back_one, axis=(0, 1)),
            jnp.sum(seq_grad * seq_gated, axis=(0, 1)),
        ]
    )
    grad_proj_low = jnp.concatenate(
        [grad_gated * x_part, grad_c, grad_gated * b_part], axis=1
    ).astype(jnp.bfloat16)
    grad_win = dot_first(normed_one, grad_proj_low).reshape(model_width, 3, channels)
    back_first = lax.psum_scatter(
        dot_last(grad_proj_low, in_flat), "tensor", scatter_dimension=0, tiled=True
    )
    grad_gain_one = jnp.sum(back_first * unit_one, axis=0)
    grad_tokens = grad_resid + norm_back(back_first, unit_one, scale_one, gain_mix)
    grad_win, grad_taps, grad_wout, grad_wgate, grad_wup, grad_down = lax.psum(
        (grad_win, grad_taps, grad_wout, grad_wgate, grad_wup, grad_down), "dp"
    )
    grad_gain_one, grad_gain_two = lax.psum((grad_gain_one, grad_gain_two), ("dp", "tensor"))
    return (
        result,
        grad_tokens,
        grad_win,
        grad_taps,
        grad_wout,
        grad_wgate,
        grad_wup,
        grad_down,
        grad_gain_one,
        grad_gain_two,
    )


def swap(values, axis, step):
    count = lax.axis_size(axis)
    return lax.ppermute(values, axis, [(i, i ^ step) for i in range(count)])


def part(values, index):
    size = values.shape[0] // 2
    return lax.dynamic_slice_in_dim(values, index * size, size, axis=0)


def in_order(bit, mine, other):
    return jnp.concatenate(
        [jnp.where(bit == 0, mine, other), jnp.where(bit == 0, other, mine)], axis=0
    )


class Sum:
    def __init__(self, values):
        rows = values.shape[0]
        cut = max(rows * 5 // 8 // 128, 1) * 128
        low = values.astype(jnp.bfloat16)
        self.place = lax.axis_index("dp")
        self.pieces = [low[:cut], low[cut:]]
        self.sent = None
        self.stage = 0
        self.start()

    def bit(self, step):
        return (self.place // step) % 2

    def steps(self):
        return {0: (1, 2), 1: (2, 1), 2: (4,), 3: (4,), 4: (2, 1), 5: (1, 2)}[self.stage]

    def start(self):
        steps = self.steps()
        if self.stage == 2:
            self.pieces = [jnp.concatenate(self.pieces, axis=0)]
        out = self.pieces
        if self.stage < 3:
            out = [part(p, 1 - self.bit(step)) for p, step in zip(out, steps)]
        self.sent = [swap(p, "dp", step) for p, step in zip(out, steps)]

    def advance(self, after=None):
        steps = self.steps()
        arrived = self.sent
        if after is not None:
            arrived = tied(arrived, after)
        if self.stage < 3:
            self.pieces = [
                (
                    part(p, self.bit(step)).astype(jnp.float32) + got.astype(jnp.float32)
                ).astype(jnp.bfloat16)
                for p, got, step in zip(self.pieces, arrived, steps)
            ]
        else:
            self.pieces = [
                in_order(self.bit(step), p, got)
                for p, got, step in zip(self.pieces, arrived, steps)
            ]
        if self.stage == 2:
            self.cut = self.sizes[0]
        if self.stage == 3:
            whole = self.pieces[0]
            self.pieces = [whole[: self.cut], whole[self.cut :]]
        if self.stage == 1:
            self.sizes = [p.shape[0] for p in self.pieces]
        self.stage += 1
        if self.stage < 6:
            self.start()

    def finish(self):
        while self.stage < 6:
            self.advance()
        return jnp.concatenate(self.pieces, axis=0).astype(jnp.float32)


def small_sum(values, axis):
    step = 1
    while step < lax.axis_size(axis):
        values = values + swap(values, axis, step)
        step *= 2
    return values


def tied(values, after):
    return lax.optimization_barrier((values, after))[0]


def gather_pair(own, core):
    return in_order(core, own, swap(own, "tensor", 1)), swap(own, "tensor", 2)


def gather_far(across, core, after):
    across = tied(across, after)
    return in_order(core, across, swap(across, "tensor", 1))


def sum_far(far, core):
    arrived = swap(part(far, 1 - core), "tensor", 1)
    return (part(far, core).astype(jnp.float32) + arrived.astype(jnp.float32)).astype(jnp.bfloat16)


def reduce_far(far, core):
    return swap(sum_far(far, core), "tensor", 2)


def reduce_near(near, core, crossed):
    arrived = swap(part(near, 1 - core), "tensor", 1)
    return (
        part(near, core).astype(jnp.float32)
        + arrived.astype(jnp.float32)
        + crossed.astype(jnp.float32)
    )


def dot(left, right):
    return jnp.dot(left, right, preferred_element_type=jnp.float32)


def down(values, shift_by):
    return jnp.pad(values, ((shift_by, 0), (0, 0)))[: values.shape[0]]


def up(values, shift_by):
    return jnp.pad(values, ((0, shift_by), (0, 0)))[shift_by:]


def conv_forward(normed, in_flat, taps):
    channels = taps.shape[1]
    projected = dot(normed, in_flat)
    b_part = projected[:, :channels]
    c_part = projected[:, channels : 2 * channels]
    x_part = projected[:, 2 * channels :]
    gated = b_part * x_part
    convolved = taps[0] * down(gated, 2) + taps[1] * down(gated, 1) + taps[2] * gated
    mixed = (c_part * convolved).astype(jnp.bfloat16)
    return mixed, (b_part, c_part, x_part, gated, convolved)


def conv_backward(grad_mixed, kept, w_out, taps):
    b_part, c_part, x_part, gated, convolved = kept
    grad_conv_out = dot_last(grad_mixed, w_out)
    grad_c = grad_conv_out * convolved
    grad_conv = grad_conv_out * c_part
    grad_gated = taps[0] * up(grad_conv, 2) + taps[1] * up(grad_conv, 1) + taps[2] * grad_conv
    grad_taps = jnp.stack(
        [
            jnp.sum(grad_conv * down(gated, 2), axis=0),
            jnp.sum(grad_conv * down(gated, 1), axis=0),
            jnp.sum(grad_conv * gated, axis=0),
        ]
    )
    grad_projected = jnp.concatenate(
        [grad_gated * x_part, grad_c, grad_gated * b_part], axis=1
    ).astype(jnp.bfloat16)
    return grad_projected, grad_taps


def mlp_forward(normed, w_gate, w_up):
    gate_pre = dot(normed, w_gate)
    up_pre = dot(normed, w_up)
    sig_gate = jax.nn.sigmoid(gate_pre)
    hidden = (gate_pre * sig_gate * up_pre).astype(jnp.bfloat16)
    return hidden, (gate_pre, up_pre, sig_gate)


def mlp_backward(grad_out, kept, w_gate, w_up, w_down):
    gate_pre, up_pre, sig_gate = kept
    grad_hidden = dot_last(grad_out, w_down)
    grad_gate = (grad_hidden * up_pre * sig_gate * (1.0 + gate_pre * (1.0 - sig_gate))).astype(
        jnp.bfloat16
    )
    grad_up = (grad_hidden * gate_pre * sig_gate).astype(jnp.bfloat16)
    back = (dot_last(grad_gate, w_gate) + dot_last(grad_up, w_up)).astype(jnp.bfloat16)
    return grad_gate, grad_up, back


def pair_shards(
    tokens, w_in, conv_kernel, w_out, w_gate, w_up, w_down, gain_mix, gain_mlp, cotangent
):
    low = jnp.bfloat16
    model_width = tokens.shape[1]
    channels = conv_kernel.shape[1]
    core = lax.axis_index("tensor") % 2
    in_flat = w_in.reshape(model_width, 3 * channels)
    taps = conv_kernel.astype(jnp.float32)
    inputs = tokens.astype(jnp.float32)
    unit_one, scale_one = rms_scale(inputs)
    one_near, across = gather_pair((unit_one * gain_mix).astype(low), core)
    mixed_near, kept_near = conv_forward(one_near, in_flat, taps)
    branch_near = dot(mixed_near, w_out).astype(low)
    one_far = gather_far(across, core, branch_near)
    mixed_far, kept_far = conv_forward(one_far, in_flat, taps)
    branch_sum = sum_far(dot(mixed_far, w_out).astype(low), core)
    crossed = swap(branch_sum, "tensor", 2)
    resid = inputs + reduce_near(branch_near, core, crossed)
    unit_two, scale_two = rms_scale(resid)
    two_near, across = gather_pair((unit_two * gain_mlp).astype(low), core)
    cot_near = in_order(core, cotangent, swap(cotangent, "tensor", 1))
    cot_across = swap(tied(cotangent, across), "tensor", 2)
    hidden_near, mlp_near = mlp_forward(two_near, w_gate, w_up)
    gate_near, up_near, back_near = mlp_backward(cot_near, mlp_near, w_gate, w_up, w_down)
    two_far = gather_far(across, core, back_near)
    hidden_far, mlp_far = mlp_forward(two_far, w_gate, w_up)
    cot_far = gather_far(cot_across, core, hidden_far)
    grad_down = (dot_first(hidden_near, cot_near) + dot_first(hidden_far, cot_far)).astype(low)
    sum_down = Sum(grad_down)
    gate_far, up_far, back_far = mlp_backward(
        tied(cot_far, grad_down), mlp_far, w_gate, w_up, w_down
    )
    back_sum = sum_far(back_far, core)
    back_crossed = swap(back_sum, "tensor", 2)
    sum_down.advance(after=back_sum)
    gate_far, up_far = tied((gate_far, up_far), back_sum)
    grad_gate = (dot_first(two_near, gate_near) + dot_first(two_far, gate_far)).astype(low)
    sum_gate = Sum(grad_gate)
    grad_up = (dot_first(two_near, up_near) + dot_first(two_far, up_far)).astype(low)
    sum_up = Sum(grad_up)
    sum_down.advance(after=grad_up)
    back_rows = reduce_near(back_near, core, tied(back_crossed, grad_up))
    grad_resid = cotangent.astype(jnp.float32) + norm_back(back_rows, unit_two, scale_two, gain_mlp)
    gain_two = jnp.sum(back_rows * unit_two, axis=0)
    gm_near, across = gather_pair(grad_resid.astype(low), core)
    gp_near, taps_near = conv_backward(gm_near, kept_near, w_out, taps)
    first_near = dot_last(gp_near, in_flat).astype(low)
    sum_down.advance(after=first_near)
    sum_gate.advance(after=first_near)
    gm_far = gather_far(across, core, first_near)
    gp_far, taps_far = conv_backward(gm_far, kept_far, w_out, taps)
    first_sum = sum_far(dot_last(gp_far, in_flat).astype(low), core)
    first_crossed = swap(first_sum, "tensor", 2)
    sum_down.advance(after=first_sum)
    sum_up.advance(after=first_sum)
    sum_gate.advance(after=first_sum)
    gp_far = tied(gp_far, first_sum)
    grad_conv = jnp.concatenate(
        [
            dot_first(one_near, gp_near) + dot_first(one_far, gp_far),
            dot_first(gm_near, mixed_near) + dot_first(gm_far, mixed_far),
        ],
        axis=1,
    ).astype(low)
    sum_conv = Sum(grad_conv)
    sum_up.advance(after=grad_conv)
    sum_down.advance(after=grad_conv)
    back_first = reduce_near(first_near, core, tied(first_crossed, sum_up.pieces))
    gain_one = jnp.sum(back_first * unit_one, axis=0)
    grad_tokens = grad_resid + norm_back(back_first, unit_one, scale_one, gain_mix)
    gains = small_sum(jnp.stack([gain_one, gain_two]), "tensor")
    small = jnp.concatenate([gains.reshape(-1), (taps_near + taps_far).reshape(-1)])
    out_near = dot(hidden_near, w_down).astype(low)
    out_far = dot(hidden_far, w_down).astype(low)
    done = (sum_up.pieces, sum_down.pieces)
    step = 1
    for each in (
        sum_gate, sum_up, sum_conv, sum_down, sum_gate, None, sum_up, sum_conv, None, sum_gate,
        sum_up, sum_conv, None, sum_gate, sum_up, sum_conv, sum_conv, sum_conv,
    ):
        if each is None:
            small = small + swap(tied(small, done), "dp", step)
            step *= 2
            done = small
            if step == 2:
                out_sum = sum_far(tied(out_far, done), core)
                out_crossed = swap(out_sum, "tensor", 2)
        else:
            each.advance(after=done)
            done = each.pieces
    result = resid + reduce_near(tied(out_near, out_crossed), core, out_crossed)
    grad_down, grad_wgate, grad_wup, grad_conv = (
        each.finish() for each in (sum_down, sum_gate, sum_up, sum_conv)
    )
    grad_win = grad_conv[:, : 3 * channels]
    grad_wout = grad_conv[:, 3 * channels :].T
    return (
        result,
        grad_tokens,
        grad_win.reshape(model_width, 3, channels),
        small[2 * model_width :].reshape(3, channels),
        grad_wout,
        grad_wgate,
        grad_wup,
        grad_down,
        small[:model_width],
        small[model_width : 2 * model_width],
    )


def solution(mesh):
    placed = (
        P(("dp", "tensor"), None),
        P(None, None, "tensor"),
        P(None, "tensor"),
        P("tensor", None),
        P(None, "tensor"),
        P(None, "tensor"),
        P("tensor", None),
        P(),
        P(),
        P(("dp", "tensor"), None),
    )
    paired = mesh.shape["tensor"] == 4 and mesh.shape["dp"] == 8
    return jax.shard_map(
        pair_shards if paired else shards,
        mesh=mesh,
        in_specs=placed,
        out_specs=(
            P(("dp", "tensor"), None),
            P(("dp", "tensor"), None),
            P(None, None, "tensor"),
            P(None, "tensor"),
            P("tensor", None),
            P(None, "tensor"),
            P(None, "tensor"),
            P("tensor", None),
            P(),
            P(),
        ),
        check_vma=False,
    )
```

```python
import jax
import jax.numpy as jnp
from jax import lax
from jax.sharding import PartitionSpec as P

LEN = 1024


EPSILON = 1e-05


def rms_scale(values):
    scale = lax.rsqrt(jnp.mean(values * values, axis=-1, keepdims=True) + EPSILON)
    return (values * scale, scale)


def norm_back(grad_norm, unit, scale, gain):
    weighted = grad_norm * gain
    return scale * (weighted - unit * jnp.mean(weighted * unit, axis=-1, keepdims=True))


def shift_down(values, shift_by):
    return jnp.pad(values, ((0, 0), (shift_by, 0), (0, 0)))[:, : values.shape[1], :]


def shift_up(values, shift_by):
    return jnp.pad(values, ((0, 0), (0, shift_by), (0, 0)))[:, shift_by:, :]


def dot_first(left, right):
    return lax.dot_general(
        left, right, (((0,), (0,)), ((), ())), preferred_element_type=jnp.float32
    )


def dot_last(left, right):
    return lax.dot_general(
        left, right, (((1,), (1,)), ((), ())), preferred_element_type=jnp.float32
    )


def shards(tokens, w_in, conv_kernel, w_out, w_gate, w_up, w_down, gain_mix, gain_mlp, cotangent):
    model_width = tokens.shape[1]
    channels = conv_kernel.shape[1]
    in_flat = w_in.reshape(model_width, 3 * channels)
    taps = conv_kernel.astype(jnp.float32)
    inputs = tokens.astype(jnp.float32)
    unit_one, scale_one = rms_scale(inputs)
    normed_one = lax.all_gather(
        (unit_one * gain_mix).astype(jnp.bfloat16), "tensor", axis=0, tiled=True
    )
    projected = jnp.dot(normed_one, in_flat, preferred_element_type=jnp.float32)
    b_part = projected[:, :channels]
    c_part = projected[:, channels : 2 * channels]
    x_part = projected[:, 2 * channels :]
    seq_gated = (b_part * x_part).reshape(-1, LEN, channels)
    back_one = shift_down(seq_gated, 1)
    back_two = shift_down(seq_gated, 2)
    convolved = (taps[0] * back_two + taps[1] * back_one + taps[2] * seq_gated).reshape(
        -1, channels
    )
    mixed_low = (c_part * convolved).astype(jnp.bfloat16)
    resid = inputs + lax.psum_scatter(
        jnp.dot(mixed_low, w_out, preferred_element_type=jnp.float32),
        "tensor",
        scatter_dimension=0,
        tiled=True,
    )
    unit_two, scale_two = rms_scale(resid)
    normed_two = lax.all_gather(
        (unit_two * gain_mlp).astype(jnp.bfloat16), "tensor", axis=0, tiled=True
    )
    gate_pre = jnp.dot(normed_two, w_gate, preferred_element_type=jnp.float32)
    up_pre = jnp.dot(normed_two, w_up, preferred_element_type=jnp.float32)
    sig_gate = jax.nn.sigmoid(gate_pre)
    activated = gate_pre * sig_gate
    hidden_low = (activated * up_pre).astype(jnp.bfloat16)
    result = resid + lax.psum_scatter(
        jnp.dot(hidden_low, w_down, preferred_element_type=jnp.float32).astype(jnp.bfloat16),
        "tensor",
        scatter_dimension=0,
        tiled=True,
    ).astype(jnp.float32)
    grad_full = lax.all_gather(cotangent, "tensor", axis=0, tiled=True)
    grad_down = dot_first(hidden_low, grad_full)
    grad_hidden = dot_last(grad_full, w_down)
    grad_gate_low = (grad_hidden * up_pre * sig_gate * (1.0 + gate_pre * (1.0 - sig_gate))).astype(
        jnp.bfloat16
    )
    grad_up_low = (grad_hidden * activated).astype(jnp.bfloat16)
    grad_wgate = dot_first(normed_two, grad_gate_low)
    grad_wup = dot_first(normed_two, grad_up_low)
    back_rows = lax.psum_scatter(
        dot_last(grad_gate_low, w_gate) + dot_last(grad_up_low, w_up),
        "tensor",
        scatter_dimension=0,
        tiled=True,
    )
    grad_resid = cotangent.astype(jnp.float32) + norm_back(back_rows, unit_two, scale_two, gain_mlp)
    grad_gain_two = jnp.sum(back_rows * unit_two, axis=0)
    grad_mixed = lax.all_gather(grad_resid.astype(jnp.bfloat16), "tensor", axis=0, tiled=True)
    grad_wout = dot_first(mixed_low, grad_mixed)
    grad_conv_out = dot_last(grad_mixed, w_out)
    grad_c = grad_conv_out * convolved
    seq_grad = (grad_conv_out * c_part).reshape(-1, LEN, channels)
    grad_gated = (
        taps[0] * shift_up(seq_grad, 2) + taps[1] * shift_up(seq_grad, 1) + taps[2] * seq_grad
    ).reshape(-1, channels)
    grad_taps = jnp.stack(
        [
            jnp.sum(seq_grad * back_two, axis=(0, 1)),
            jnp.sum(seq_grad * back_one, axis=(0, 1)),
            jnp.sum(seq_grad * seq_gated, axis=(0, 1)),
        ]
    )
    grad_proj_low = jnp.concatenate(
        [grad_gated * x_part, grad_c, grad_gated * b_part], axis=1
    ).astype(jnp.bfloat16)
    grad_win = dot_first(normed_one, grad_proj_low).reshape(model_width, 3, channels)
    back_first = lax.psum_scatter(
        dot_last(grad_proj_low, in_flat), "tensor", scatter_dimension=0, tiled=True
    )
    grad_gain_one = jnp.sum(back_first * unit_one, axis=0)
    grad_tokens = grad_resid + norm_back(back_first, unit_one, scale_one, gain_mix)
    grad_win, grad_taps, grad_wout, grad_wgate, grad_wup, grad_down = lax.psum(
        (grad_win, grad_taps, grad_wout, grad_wgate, grad_wup, grad_down), "dp"
    )
    grad_gain_one, grad_gain_two = lax.psum((grad_gain_one, grad_gain_two), ("dp", "tensor"))
    return (
        result,
        grad_tokens,
        grad_win,
        grad_taps,
        grad_wout,
        grad_wgate,
        grad_wup,
        grad_down,
        grad_gain_one,
        grad_gain_two,
    )


def swap(values, axis, step):
    count = lax.axis_size(axis)
    return lax.ppermute(values, axis, [(i, i ^ step) for i in range(count)])


def part(values, index):
    size = values.shape[0] // 2
    return lax.dynamic_slice_in_dim(values, index * size, size, axis=0)


def in_order(bit, mine, other):
    return jnp.concatenate(
        [jnp.where(bit == 0, mine, other), jnp.where(bit == 0, other, mine)], axis=0
    )


class Sum:
    def __init__(self, *pieces):
        self.place = lax.axis_index("dp")
        self.pieces = list(pieces)
        self.sent = None
        self.stage = 0
        self.start()

    def bit(self, step):
        return (self.place // step) % 2

    def steps(self):
        return {0: (1, 2), 1: (2, 1), 2: (4,), 3: (4,), 4: (2, 1), 5: (1, 2)}[self.stage]

    def start(self):
        steps = self.steps()
        if self.stage == 2:
            self.pieces = [jnp.concatenate(self.pieces, axis=0)]
        out = self.pieces
        if self.stage < 3:
            out = [part(p, 1 - self.bit(step)) for p, step in zip(out, steps)]
        self.sent = [swap(p, "dp", step) for p, step in zip(out, steps)]

    def advance(self, after=None):
        steps = self.steps()
        arrived = self.sent
        if after is not None:
            arrived = tied(arrived, after)
        if self.stage < 3:
            self.pieces = [
                (
                    part(p, self.bit(step)).astype(jnp.float32) + got.astype(jnp.float32)
                ).astype(jnp.bfloat16)
                for p, got, step in zip(self.pieces, arrived, steps)
            ]
        else:
            self.pieces = [
                in_order(self.bit(step), p, got)
                for p, got, step in zip(self.pieces, arrived, steps)
            ]
        if self.stage == 2:
            self.cut = self.sizes[0]
        if self.stage == 3:
            whole = self.pieces[0]
            self.pieces = [whole[: self.cut], whole[self.cut :]]
        if self.stage == 1:
            self.sizes = [p.shape[0] for p in self.pieces]
        self.stage += 1
        if self.stage < 6:
            self.start()

    def finish(self):
        while self.stage < 6:
            self.advance()
        return [piece.astype(jnp.float32) for piece in self.pieces]


def small_sum(values, axis):
    step = 1
    while step < lax.axis_size(axis):
        values = values + swap(values, axis, step)
        step *= 2
    return values


def tied(values, after):
    return lax.optimization_barrier((values, after))[0]


def gather_pair(own, core):
    return in_order(core, own, swap(own, "tensor", 1)), swap(own, "tensor", 2)


def gather_far(across, core, after):
    across = tied(across, after)
    return in_order(core, across, swap(across, "tensor", 1))


def sum_far(far, core):
    arrived = swap(part(far, 1 - core), "tensor", 1)
    return (part(far, core).astype(jnp.float32) + arrived.astype(jnp.float32)).astype(jnp.bfloat16)


def reduce_far(far, core):
    return swap(sum_far(far, core), "tensor", 2)


def reduce_near(near, core, crossed):
    arrived = swap(part(near, 1 - core), "tensor", 1)
    return (
        part(near, core).astype(jnp.float32)
        + arrived.astype(jnp.float32)
        + crossed.astype(jnp.float32)
    )


def dot(left, right):
    return jnp.dot(left, right, preferred_element_type=jnp.float32)


def down(values, shift_by):
    return jnp.pad(values, ((shift_by, 0), (0, 0)))[: values.shape[0]]


def up(values, shift_by):
    return jnp.pad(values, ((0, shift_by), (0, 0)))[shift_by:]


def conv_forward(normed, in_flat, taps):
    channels = taps.shape[1]
    projected = dot(normed, in_flat)
    b_part = projected[:, :channels]
    c_part = projected[:, channels : 2 * channels]
    x_part = projected[:, 2 * channels :]
    gated = b_part * x_part
    convolved = taps[0] * down(gated, 2) + taps[1] * down(gated, 1) + taps[2] * gated
    mixed = (c_part * convolved).astype(jnp.bfloat16)
    return mixed, (b_part, c_part, x_part, gated, convolved)


def conv_backward(grad_mixed, kept, w_out, taps):
    b_part, c_part, x_part, gated, convolved = kept
    grad_conv_out = dot_last(grad_mixed, w_out)
    grad_c = grad_conv_out * convolved
    grad_conv = grad_conv_out * c_part
    grad_gated = taps[0] * up(grad_conv, 2) + taps[1] * up(grad_conv, 1) + taps[2] * grad_conv
    grad_taps = jnp.stack(
        [
            jnp.sum(grad_conv * down(gated, 2), axis=0),
            jnp.sum(grad_conv * down(gated, 1), axis=0),
            jnp.sum(grad_conv * gated, axis=0),
        ]
    )
    grad_projected = jnp.concatenate(
        [grad_gated * x_part, grad_c, grad_gated * b_part], axis=1
    ).astype(jnp.bfloat16)
    return grad_projected, grad_taps


def mlp_forward(normed, w_gate, w_up):
    gate_pre = dot(normed, w_gate)
    up_pre = dot(normed, w_up)
    sig_gate = jax.nn.sigmoid(gate_pre)
    hidden = (gate_pre * sig_gate * up_pre).astype(jnp.bfloat16)
    return hidden, (gate_pre, up_pre, sig_gate)


def mlp_backward(grad_out, kept, w_gate, w_up, w_down):
    gate_pre, up_pre, sig_gate = kept
    grad_hidden = dot_last(grad_out, w_down)
    grad_gate = (grad_hidden * up_pre * sig_gate * (1.0 + gate_pre * (1.0 - sig_gate))).astype(
        jnp.bfloat16
    )
    grad_up = (grad_hidden * gate_pre * sig_gate).astype(jnp.bfloat16)
    back = (dot_last(grad_gate, w_gate) + dot_last(grad_up, w_up)).astype(jnp.bfloat16)
    return grad_gate, grad_up, back


def pair_shards(
    tokens, w_in, conv_kernel, w_out, w_gate, w_up, w_down, gain_mix, gain_mlp, cotangent
):
    low = jnp.bfloat16
    model_width = tokens.shape[1]
    channels = conv_kernel.shape[1]
    core = lax.axis_index("tensor") % 2
    in_flat = w_in.reshape(model_width, 3 * channels)
    taps = conv_kernel.astype(jnp.float32)
    inputs = tokens.astype(jnp.float32)
    unit_one, scale_one = rms_scale(inputs)
    one_near, across = gather_pair((unit_one * gain_mix).astype(low), core)
    mixed_near, kept_near = conv_forward(one_near, in_flat, taps)
    branch_near = dot(mixed_near, w_out).astype(low)
    one_far = gather_far(across, core, branch_near)
    mixed_far, kept_far = conv_forward(one_far, in_flat, taps)
    branch_sum = sum_far(dot(mixed_far, w_out).astype(low), core)
    crossed = swap(branch_sum, "tensor", 2)
    resid = inputs + reduce_near(branch_near, core, crossed)
    unit_two, scale_two = rms_scale(resid)
    two_near, across = gather_pair((unit_two * gain_mlp).astype(low), core)
    cot_near = in_order(core, cotangent, swap(cotangent, "tensor", 1))
    cot_across = swap(tied(cotangent, across), "tensor", 2)
    hidden_near, mlp_near = mlp_forward(two_near, w_gate, w_up)
    gate_near, up_near, back_near = mlp_backward(cot_near, mlp_near, w_gate, w_up, w_down)
    two_far = gather_far(across, core, back_near)
    hidden_far, mlp_far = mlp_forward(two_far, w_gate, w_up)
    out_far = dot(hidden_far, w_down).astype(low)
    out_sum = sum_far(out_far, core)
    down_near = dot_first(hidden_near, cot_near)
    wgate_near = dot_first(two_near, gate_near)
    wup_near = dot_first(two_near, up_near)
    out_near = dot(hidden_near, w_down).astype(low)
    cot_far = gather_far(cot_across, core, (out_sum, down_near, wgate_near, wup_near, out_near))
    grad_down = (down_near + dot_first(hidden_far, cot_far)).astype(low)
    cut = grad_down.shape[0] // 2 // 128 * 128 + 256
    sum_down = Sum(grad_down[:cut], grad_down[cut:])
    gate_far, up_far, back_far = mlp_backward(
        tied(cot_far, grad_down), mlp_far, w_gate, w_up, w_down
    )
    back_sum = sum_far(back_far, core)
    back_crossed = swap(back_sum, "tensor", 2)
    sum_down.advance(after=back_sum)
    gate_far, up_far = tied((gate_far, up_far), back_sum)
    grad_gate = (wgate_near + dot_first(two_far, gate_far)).astype(low)
    grad_up = (wup_near + dot_first(two_far, up_far)).astype(low)
    sum_mlp = Sum(grad_gate, grad_up)
    sum_down.advance(after=grad_up)
    back_rows = reduce_near(tied(back_near, grad_gate), core, tied(back_crossed, grad_up))
    grad_resid = cotangent.astype(jnp.float32) + norm_back(back_rows, unit_two, scale_two, gain_mlp)
    gain_two = jnp.sum(back_rows * unit_two, axis=0)
    gm_near, across = gather_pair(grad_resid.astype(low), core)
    gp_near, taps_near = conv_backward(gm_near, kept_near, w_out, taps)
    first_near = dot_last(gp_near, in_flat).astype(low)
    sum_down.advance(after=first_near)
    sum_mlp.advance(after=first_near)
    gm_far = gather_far(across, core, first_near)
    gp_far, taps_far = conv_backward(gm_far, kept_far, w_out, taps)
    first_sum = sum_far(dot_last(gp_far, in_flat).astype(low), core)
    first_crossed = swap(first_sum, "tensor", 2)
    sum_down.advance(after=first_sum)
    gp_far = tied(gp_far, first_sum)
    grad_blocks = jnp.concatenate(
        [
            dot_first(one_near, gp_near[:, i * channels : (i + 1) * channels])
            + dot_first(one_far, gp_far[:, i * channels : (i + 1) * channels])
            for i in range(3)
        ],
        axis=0,
    ).astype(low)
    grad_wout = (dot_first(gm_near, mixed_near) + dot_first(gm_far, mixed_far)).astype(low)
    sum_conv = Sum(grad_blocks, grad_wout)
    sum_mlp.advance(after=grad_blocks)
    sum_down.advance(after=grad_blocks)
    back_first = reduce_near(tied(first_near, grad_wout), core, tied(first_crossed, sum_mlp.pieces))
    gain_one = jnp.sum(back_first * unit_one, axis=0)
    grad_tokens = grad_resid + norm_back(back_first, unit_one, scale_one, gain_mix)
    gains = small_sum(jnp.stack([gain_one, gain_two]), "tensor")
    out_crossed = swap(tied(out_sum, first_crossed), "tensor", 2)
    small = jnp.concatenate([gains.reshape(-1), (taps_near + taps_far).reshape(-1)])
    done = (sum_mlp.pieces, sum_down.pieces)
    step = 1
    for each in (
        sum_mlp, sum_conv, sum_down, None, sum_conv, sum_mlp, None, sum_conv, sum_mlp, None,
        sum_conv, sum_mlp, sum_conv, sum_conv,
    ):
        if each is sum_mlp and each.stage == 4:
            result = resid + reduce_near(tied(out_near, done), core, out_crossed)
            done = result
        if each is None:
            small = small + swap(tied(small, done), "dp", step)
            step *= 2
            done = small
        else:
            each.advance(after=done)
            done = each.pieces
    grad_down = jnp.concatenate(sum_down.finish(), axis=0)
    grad_wgate, grad_wup = sum_mlp.finish()
    grad_blocks, grad_wout = sum_conv.finish()
    grad_win = grad_blocks.reshape(3, model_width, channels).transpose(1, 0, 2)
    grad_wout = grad_wout.T
    return (
        result,
        grad_tokens,
        grad_win,
        small[2 * model_width :].reshape(3, channels),
        grad_wout,
        grad_wgate,
        grad_wup,
        grad_down,
        small[:model_width],
        small[model_width : 2 * model_width],
    )


def solution(mesh):
    placed = (
        P(("dp", "tensor"), None),
        P(None, None, "tensor"),
        P(None, "tensor"),
        P("tensor", None),
        P(None, "tensor"),
        P(None, "tensor"),
        P("tensor", None),
        P(),
        P(),
        P(("dp", "tensor"), None),
    )
    paired = mesh.shape["tensor"] == 4 and mesh.shape["dp"] == 8
    return jax.shard_map(
        pair_shards if paired else shards,
        mesh=mesh,
        in_specs=placed,
        out_specs=(
            P(("dp", "tensor"), None),
            P(("dp", "tensor"), None),
            P(None, None, "tensor"),
            P(None, "tensor"),
            P("tensor", None),
            P(None, "tensor"),
            P(None, "tensor"),
            P("tensor", None),
            P(),
            P(),
        ),
        check_vma=False,
    )
```

```python
import jax
import jax.numpy as jnp
from jax import lax
from jax.sharding import PartitionSpec as P

LEN = 1024


EPSILON = 1e-05


def rms_scale(values):
    scale = lax.rsqrt(jnp.mean(values * values, axis=-1, keepdims=True) + EPSILON)
    return (values * scale, scale)


def norm_back(grad_norm, unit, scale, gain):
    weighted = grad_norm * gain
    return scale * (weighted - unit * jnp.mean(weighted * unit, axis=-1, keepdims=True))


def shift_down(values, shift_by):
    return jnp.pad(values, ((0, 0), (shift_by, 0), (0, 0)))[:, : values.shape[1], :]


def shift_up(values, shift_by):
    return jnp.pad(values, ((0, 0), (0, shift_by), (0, 0)))[:, shift_by:, :]


def dot_first(left, right):
    return lax.dot_general(
        left, right, (((0,), (0,)), ((), ())), preferred_element_type=jnp.float32
    )


def dot_last(left, right):
    return lax.dot_general(
        left, right, (((1,), (1,)), ((), ())), preferred_element_type=jnp.float32
    )


def shards(tokens, w_in, conv_kernel, w_out, w_gate, w_up, w_down, gain_mix, gain_mlp, cotangent):
    model_width = tokens.shape[1]
    channels = conv_kernel.shape[1]
    in_flat = w_in.reshape(model_width, 3 * channels)
    taps = conv_kernel.astype(jnp.float32)
    inputs = tokens.astype(jnp.float32)
    unit_one, scale_one = rms_scale(inputs)
    normed_one = lax.all_gather(
        (unit_one * gain_mix).astype(jnp.bfloat16), "tensor", axis=0, tiled=True
    )
    projected = jnp.dot(normed_one, in_flat, preferred_element_type=jnp.float32)
    b_part = projected[:, :channels]
    c_part = projected[:, channels : 2 * channels]
    x_part = projected[:, 2 * channels :]
    seq_gated = (b_part * x_part).reshape(-1, LEN, channels)
    back_one = shift_down(seq_gated, 1)
    back_two = shift_down(seq_gated, 2)
    convolved = (taps[0] * back_two + taps[1] * back_one + taps[2] * seq_gated).reshape(
        -1, channels
    )
    mixed_low = (c_part * convolved).astype(jnp.bfloat16)
    resid = inputs + lax.psum_scatter(
        jnp.dot(mixed_low, w_out, preferred_element_type=jnp.float32),
        "tensor",
        scatter_dimension=0,
        tiled=True,
    )
    unit_two, scale_two = rms_scale(resid)
    normed_two = lax.all_gather(
        (unit_two * gain_mlp).astype(jnp.bfloat16), "tensor", axis=0, tiled=True
    )
    gate_pre = jnp.dot(normed_two, w_gate, preferred_element_type=jnp.float32)
    up_pre = jnp.dot(normed_two, w_up, preferred_element_type=jnp.float32)
    sig_gate = jax.nn.sigmoid(gate_pre)
    activated = gate_pre * sig_gate
    hidden_low = (activated * up_pre).astype(jnp.bfloat16)
    result = resid + lax.psum_scatter(
        jnp.dot(hidden_low, w_down, preferred_element_type=jnp.float32).astype(jnp.bfloat16),
        "tensor",
        scatter_dimension=0,
        tiled=True,
    ).astype(jnp.float32)
    grad_full = lax.all_gather(cotangent, "tensor", axis=0, tiled=True)
    grad_down = dot_first(hidden_low, grad_full)
    grad_hidden = dot_last(grad_full, w_down)
    grad_gate_low = (grad_hidden * up_pre * sig_gate * (1.0 + gate_pre * (1.0 - sig_gate))).astype(
        jnp.bfloat16
    )
    grad_up_low = (grad_hidden * activated).astype(jnp.bfloat16)
    grad_wgate = dot_first(normed_two, grad_gate_low)
    grad_wup = dot_first(normed_two, grad_up_low)
    back_rows = lax.psum_scatter(
        dot_last(grad_gate_low, w_gate) + dot_last(grad_up_low, w_up),
        "tensor",
        scatter_dimension=0,
        tiled=True,
    )
    grad_resid = cotangent.astype(jnp.float32) + norm_back(back_rows, unit_two, scale_two, gain_mlp)
    grad_gain_two = jnp.sum(back_rows * unit_two, axis=0)
    grad_mixed = lax.all_gather(grad_resid.astype(jnp.bfloat16), "tensor", axis=0, tiled=True)
    grad_wout = dot_first(mixed_low, grad_mixed)
    grad_conv_out = dot_last(grad_mixed, w_out)
    grad_c = grad_conv_out * convolved
    seq_grad = (grad_conv_out * c_part).reshape(-1, LEN, channels)
    grad_gated = (
        taps[0] * shift_up(seq_grad, 2) + taps[1] * shift_up(seq_grad, 1) + taps[2] * seq_grad
    ).reshape(-1, channels)
    grad_taps = jnp.stack(
        [
            jnp.sum(seq_grad * back_two, axis=(0, 1)),
            jnp.sum(seq_grad * back_one, axis=(0, 1)),
            jnp.sum(seq_grad * seq_gated, axis=(0, 1)),
        ]
    )
    grad_proj_low = jnp.concatenate(
        [grad_gated * x_part, grad_c, grad_gated * b_part], axis=1
    ).astype(jnp.bfloat16)
    grad_win = dot_first(normed_one, grad_proj_low).reshape(model_width, 3, channels)
    back_first = lax.psum_scatter(
        dot_last(grad_proj_low, in_flat), "tensor", scatter_dimension=0, tiled=True
    )
    grad_gain_one = jnp.sum(back_first * unit_one, axis=0)
    grad_tokens = grad_resid + norm_back(back_first, unit_one, scale_one, gain_mix)
    grad_win, grad_taps, grad_wout, grad_wgate, grad_wup, grad_down = lax.psum(
        (grad_win, grad_taps, grad_wout, grad_wgate, grad_wup, grad_down), "dp"
    )
    grad_gain_one, grad_gain_two = lax.psum((grad_gain_one, grad_gain_two), ("dp", "tensor"))
    return (
        result,
        grad_tokens,
        grad_win,
        grad_taps,
        grad_wout,
        grad_wgate,
        grad_wup,
        grad_down,
        grad_gain_one,
        grad_gain_two,
    )


def swap(values, axis, step):
    count = lax.axis_size(axis)
    return lax.ppermute(values, axis, [(i, i ^ step) for i in range(count)])


def part(values, index):
    size = values.shape[0] // 2
    return lax.dynamic_slice_in_dim(values, index * size, size, axis=0)


def in_order(bit, mine, other):
    return jnp.concatenate(
        [jnp.where(bit == 0, mine, other), jnp.where(bit == 0, other, mine)], axis=0
    )


class Sum:
    def __init__(self, *pieces):
        self.place = lax.axis_index("dp")
        self.pieces = list(pieces)
        self.sent = None
        self.stage = 0
        self.start()

    def bit(self, step):
        return (self.place // step) % 2

    def steps(self):
        return {0: (1, 2), 1: (2, 1), 2: (4,), 3: (4,), 4: (2, 1), 5: (1, 2)}[self.stage]

    def start(self):
        steps = self.steps()
        if self.stage == 2:
            self.pieces = [jnp.concatenate(self.pieces, axis=0)]
        out = self.pieces
        if self.stage < 3:
            out = [part(p, 1 - self.bit(step)) for p, step in zip(out, steps)]
        self.sent = [swap(p, "dp", step) for p, step in zip(out, steps)]

    def advance(self, after=None):
        steps = self.steps()
        arrived = self.sent
        if after is not None:
            arrived = tied(arrived, after)
        if self.stage < 3:
            self.pieces = [
                (
                    part(p, self.bit(step)).astype(jnp.float32) + got.astype(jnp.float32)
                ).astype(jnp.bfloat16)
                for p, got, step in zip(self.pieces, arrived, steps)
            ]
        else:
            self.pieces = [
                in_order(self.bit(step), p, got)
                for p, got, step in zip(self.pieces, arrived, steps)
            ]
        if self.stage == 2:
            self.cut = self.sizes[0]
        if self.stage == 3:
            whole = self.pieces[0]
            self.pieces = [whole[: self.cut], whole[self.cut :]]
        if self.stage == 1:
            self.sizes = [p.shape[0] for p in self.pieces]
        self.stage += 1
        if self.stage < 6:
            self.start()

    def finish(self):
        while self.stage < 6:
            self.advance()
        return [piece.astype(jnp.float32) for piece in self.pieces]


def small_sum(values, axis):
    step = 1
    while step < lax.axis_size(axis):
        values = values + swap(values, axis, step)
        step *= 2
    return values


def tied(values, after):
    return lax.optimization_barrier((values, after))[0]


def gather_pair(own, core):
    return in_order(core, own, swap(own, "tensor", 1)), swap(own, "tensor", 2)


def gather_far(across, core, after):
    across = tied(across, after)
    return in_order(core, across, swap(across, "tensor", 1))


def sum_far(far, core):
    arrived = swap(part(far, 1 - core), "tensor", 1)
    return (part(far, core).astype(jnp.float32) + arrived.astype(jnp.float32)).astype(jnp.bfloat16)


def reduce_far(far, core):
    return swap(sum_far(far, core), "tensor", 2)


def reduce_near(near, core, crossed):
    arrived = swap(part(near, 1 - core), "tensor", 1)
    return (
        part(near, core).astype(jnp.float32)
        + arrived.astype(jnp.float32)
        + crossed.astype(jnp.float32)
    )


def dot(left, right):
    return jnp.dot(left, right, preferred_element_type=jnp.float32)


def down(values, shift_by):
    return jnp.pad(values, ((shift_by, 0), (0, 0)))[: values.shape[0]]


def up(values, shift_by):
    return jnp.pad(values, ((0, shift_by), (0, 0)))[shift_by:]


def conv_forward(normed, in_flat, taps):
    channels = taps.shape[1]
    projected = dot(normed, in_flat)
    b_part = projected[:, :channels]
    c_part = projected[:, channels : 2 * channels]
    x_part = projected[:, 2 * channels :]
    gated = b_part * x_part
    convolved = taps[0] * down(gated, 2) + taps[1] * down(gated, 1) + taps[2] * gated
    mixed = (c_part * convolved).astype(jnp.bfloat16)
    return mixed, (b_part, c_part, x_part, gated, convolved)


def conv_backward(grad_mixed, kept, w_out, taps):
    b_part, c_part, x_part, gated, convolved = kept
    grad_conv_out = dot_last(grad_mixed, w_out)
    grad_c = grad_conv_out * convolved
    grad_conv = grad_conv_out * c_part
    grad_gated = taps[0] * up(grad_conv, 2) + taps[1] * up(grad_conv, 1) + taps[2] * grad_conv
    grad_taps = jnp.stack(
        [
            jnp.sum(grad_conv * down(gated, 2), axis=0),
            jnp.sum(grad_conv * down(gated, 1), axis=0),
            jnp.sum(grad_conv * gated, axis=0),
        ]
    )
    grad_projected = jnp.concatenate(
        [grad_gated * x_part, grad_c, grad_gated * b_part], axis=1
    ).astype(jnp.bfloat16)
    return grad_projected, grad_taps


def mlp_forward(normed, w_gate, w_up):
    gate_pre = dot(normed, w_gate)
    up_pre = dot(normed, w_up)
    sig_gate = jax.nn.sigmoid(gate_pre)
    hidden = (gate_pre * sig_gate * up_pre).astype(jnp.bfloat16)
    return hidden, (gate_pre, up_pre, sig_gate)


def mlp_backward(grad_out, kept, w_gate, w_up, w_down):
    gate_pre, up_pre, sig_gate = kept
    grad_hidden = dot_last(grad_out, w_down)
    grad_gate = (grad_hidden * up_pre * sig_gate * (1.0 + gate_pre * (1.0 - sig_gate))).astype(
        jnp.bfloat16
    )
    grad_up = (grad_hidden * gate_pre * sig_gate).astype(jnp.bfloat16)
    back = (dot_last(grad_gate, w_gate) + dot_last(grad_up, w_up)).astype(jnp.bfloat16)
    return grad_gate, grad_up, back


def pair_shards(
    tokens, w_in, conv_kernel, w_out, w_gate, w_up, w_down, gain_mix, gain_mlp, cotangent
):
    low = jnp.bfloat16
    model_width = tokens.shape[1]
    channels = conv_kernel.shape[1]
    core = lax.axis_index("tensor") % 2
    in_flat = w_in.reshape(model_width, 3 * channels)
    taps = conv_kernel.astype(jnp.float32)
    inputs = tokens.astype(jnp.float32)
    unit_one, scale_one = rms_scale(inputs)
    one_near, across = gather_pair((unit_one * gain_mix).astype(low), core)
    mixed_near, kept_near = conv_forward(one_near, in_flat, taps)
    branch_near = dot(mixed_near, w_out).astype(low)
    one_far = gather_far(across, core, branch_near)
    mixed_far, kept_far = conv_forward(one_far, in_flat, taps)
    branch_sum = sum_far(dot(mixed_far, w_out).astype(low), core)
    crossed = swap(branch_sum, "tensor", 2)
    resid = inputs + reduce_near(branch_near, core, crossed)
    unit_two, scale_two = rms_scale(resid)
    two_near, across = gather_pair((unit_two * gain_mlp).astype(low), core)
    cot_near = in_order(core, cotangent, swap(cotangent, "tensor", 1))
    cot_across = swap(tied(cotangent, across), "tensor", 2)
    hidden_near, mlp_near = mlp_forward(two_near, w_gate, w_up)
    gate_near, up_near, back_near = mlp_backward(cot_near, mlp_near, w_gate, w_up, w_down)
    two_far = gather_far(across, core, back_near)
    hidden_far, mlp_far = mlp_forward(two_far, w_gate, w_up)
    out_far = dot(hidden_far, w_down).astype(low)
    out_sum = sum_far(out_far, core)
    down_near = dot_first(hidden_near, cot_near)
    wgate_near = dot_first(two_near, gate_near)
    wup_near = dot_first(two_near, up_near)
    out_near = dot(hidden_near, w_down).astype(low)
    cot_far = gather_far(cot_across, core, (out_sum, down_near, wgate_near, wup_near, out_near))
    grad_down = (down_near + dot_first(hidden_far, cot_far)).astype(low)
    cut = grad_down.shape[0] // 2 // 128 * 128 + 256
    sum_down = Sum(grad_down[:cut], grad_down[cut:])
    gate_far, up_far, back_far = mlp_backward(
        tied(cot_far, grad_down), mlp_far, w_gate, w_up, w_down
    )
    back_sum = sum_far(back_far, core)
    back_crossed = swap(back_sum, "tensor", 2)
    gate_far, up_far = tied((gate_far, up_far), back_sum)
    grad_gate = (wgate_near + dot_first(two_far, gate_far)).astype(low)
    grad_up = (wup_near + dot_first(two_far, up_far)).astype(low)
    sum_down.sent, grad_gate = lax.optimization_barrier((sum_down.sent, grad_gate))
    sum_down.advance()
    sum_mlp = Sum(grad_gate, grad_up)
    sum_down.advance(after=grad_up)
    back_rows = reduce_near(tied(back_near, grad_gate), core, tied(back_crossed, grad_up))
    grad_resid = cotangent.astype(jnp.float32) + norm_back(back_rows, unit_two, scale_two, gain_mlp)
    gain_two = jnp.sum(back_rows * unit_two, axis=0)
    gm_near, across = gather_pair(grad_resid.astype(low), core)
    gp_near, taps_near = conv_backward(gm_near, kept_near, w_out, taps)
    first_near = dot_last(gp_near, in_flat).astype(low)
    sum_down.advance(after=first_near)
    sum_mlp.advance(after=first_near)
    gm_far = gather_far(across, core, first_near)
    gp_far, taps_far = conv_backward(gm_far, kept_far, w_out, taps)
    first_sum = sum_far(dot_last(gp_far, in_flat).astype(low), core)
    first_crossed = swap(first_sum, "tensor", 2)
    sum_down.advance(after=first_sum)
    gp_far = tied(gp_far, first_sum)
    grad_blocks = jnp.concatenate(
        [
            dot_first(one_near, gp_near[:, i * channels : (i + 1) * channels])
            + dot_first(one_far, gp_far[:, i * channels : (i + 1) * channels])
            for i in range(3)
        ],
        axis=0,
    ).astype(low)
    grad_wout = (dot_first(gm_near, mixed_near) + dot_first(gm_far, mixed_far)).astype(low)
    sum_conv = Sum(grad_blocks, grad_wout)
    sum_mlp.advance(after=grad_blocks)
    sum_down.advance(after=grad_blocks)
    back_first = reduce_near(tied(first_near, grad_wout), core, tied(first_crossed, sum_mlp.pieces))
    gain_one = jnp.sum(back_first * unit_one, axis=0)
    grad_tokens = grad_resid + norm_back(back_first, unit_one, scale_one, gain_mix)
    gains = small_sum(jnp.stack([gain_one, gain_two]), "tensor")
    out_crossed = swap(tied(out_sum, first_crossed), "tensor", 2)
    small = jnp.concatenate([gains.reshape(-1), (taps_near + taps_far).reshape(-1)])
    last = sum_mlp
    step = 1
    for each in (
        sum_conv, sum_mlp, None, sum_down, sum_conv, sum_mlp, sum_conv, None, sum_conv, sum_mlp,
        None, sum_conv, sum_mlp, sum_conv,
    ):
        if each is None:
            small, last.pieces = lax.optimization_barrier((small, last.pieces))
            small = small + swap(small, "dp", step)
            step *= 2
            continue
        if each is sum_mlp and each.stage == 4:
            out_near, last.pieces = lax.optimization_barrier((out_near, last.pieces))
            result = resid + reduce_near(out_near, core, out_crossed)
        each.sent, last.pieces = lax.optimization_barrier((each.sent, last.pieces))
        each.advance()
        last = each
    grad_down = jnp.concatenate(sum_down.finish(), axis=0)
    grad_wgate, grad_wup = sum_mlp.finish()
    grad_blocks, grad_wout = sum_conv.finish()
    grad_win = grad_blocks.reshape(3, model_width, channels).transpose(1, 0, 2)
    grad_wout = grad_wout.T
    return (
        result,
        grad_tokens,
        grad_win,
        small[2 * model_width :].reshape(3, channels),
        grad_wout,
        grad_wgate,
        grad_wup,
        grad_down,
        small[:model_width],
        small[model_width : 2 * model_width],
    )


def solution(mesh):
    placed = (
        P(("dp", "tensor"), None),
        P(None, None, "tensor"),
        P(None, "tensor"),
        P("tensor", None),
        P(None, "tensor"),
        P(None, "tensor"),
        P("tensor", None),
        P(),
        P(),
        P(("dp", "tensor"), None),
    )
    paired = mesh.shape["tensor"] == 4 and mesh.shape["dp"] == 8
    return jax.shard_map(
        pair_shards if paired else shards,
        mesh=mesh,
        in_specs=placed,
        out_specs=(
            P(("dp", "tensor"), None),
            P(("dp", "tensor"), None),
            P(None, None, "tensor"),
            P(None, "tensor"),
            P("tensor", None),
            P(None, "tensor"),
            P(None, "tensor"),
            P("tensor", None),
            P(),
            P(),
        ),
        check_vma=False,
    )
```
